32 devices in a mesh: gene: 4 (over x, core), peak: 8 (over z, y).
Axes of the slice: x: 2, y: 2, z: 4, core: 2. Of those that a mesh axis runs over, the one named last changes fastest.
Arguments:
- gene_act: bfloat16 [4096, 1024], P('peak'), may hold values from -6 to 6
- peak_act: bfloat16 [16384, 1024], P('peak'), may hold values from -6 to 6
- w_query: bfloat16 [1024, 1024], P(None, 'gene'), may hold values from -0.1875 to 0.1875
- w_key: bfloat16 [1024, 1024], P(None, 'gene'), may hold values from -0.1875 to 0.1875
- w_value: bfloat16 [1024, 1024], P(None, 'gene'), may hold values from -0.1875 to 0.1875
- w_out: bfloat16 [1024, 1024], P('gene'), may hold values from -0.1875 to 0.1875
- head_bias: float32 [8], P('gene'), may hold values from -6 to -3
- block_mask: int32 [32, 128], replicated, may hold values from 0 to 1, as said below
- gene_chrom: int32 [4096], replicated, may hold values from 0 to 22, as said below
- peak_chrom: int32 [16384], replicated, may hold values from 0 to 22, as said below
Outputs:
- mixed: bfloat16 [4096, 1024], P('peak', 'gene')
The draws below stay inside these ranges and needn't reach their ends.
Inputs may be any that keep to these rules, and one draw needn't show every extreme that they name: For each gene tile i, the 1s of block_mask[i] form one run of consecutive peak tiles that contains tile 4i and lies within the peak tiles of the shards o - 2 to o + 2, where o = i // 4 is the shard of peak that holds gene tile i; runs of different lengths reach that limit on either side in every draw. `peak_chrom`: never falls along the peaks; each chromosome is one run of consecutive peaks. `gene_chrom`: gene query g lies at peak position 4g and carries that peak's chromosome.
All inputs are finite; a program needn't handle non-finite values.
Results may differ from the reference program's by a relative error of at most 0.0064.
Values may be sent and summed in bfloat16 or wider, within the bound.
A program may use at most 128 MiB of HBM per device.

```python
import math
import jax
import jax.numpy as jnp
from jax import lax

D = 1024
HEADS = 8
GENE_DEV = 512
PEAK_DEV = 2048
TILE = 128
REACH = 2
CHROMS = 23
GENES = 4096
PEAKS = 16384
GENE_TILES = 32
PEAK_TILES = 128
N_PEAK = 8


def chromosome_cuts(key):
    spacing = PEAKS // GENES
    return jax.random.randint(jax.random.fold_in(key, 7), (CHROMS - 1,), 1, PEAKS - spacing)


def draw_peak_chrom(key, part):
    cuts = chromosome_cuts(key)
    position = jnp.arange(PEAKS, dtype=jnp.int32)
    return jnp.sum((cuts[None, :] <= position[:, None]).astype(jnp.int32), axis=1)


def draw_gene_chrom(key, part):
    cuts = chromosome_cuts(key)
    position = jnp.arange(GENES, dtype=jnp.int32) * (PEAKS // GENES)
    return jnp.sum((cuts[None, :] <= position[:, None]).astype(jnp.int32), axis=1)


def draw_block_mask(key, part):
    per_dev = PEAK_DEV // TILE
    ratio = PEAK_TILES // GENE_TILES
    row = jnp.arange(GENE_TILES, dtype=jnp.int32)
    owner = row // (GENE_DEV // TILE)
    centre = row * ratio
    reach_low = jax.random.randint(jax.random.fold_in(key, 11), (GENE_TILES,), 0, (REACH + 1) * per_dev + 1)
    reach_high = jax.random.randint(jax.random.fold_in(key, 13), (GENE_TILES,), 0, (REACH + 1) * per_dev + 1)
    lowest = jnp.maximum(centre - reach_low, (owner - REACH) * per_dev)
    highest = jnp.minimum(centre + reach_high, (owner + REACH + 1) * per_dev - 1)
    column = jnp.arange(PEAK_TILES, dtype=jnp.int32)
    inside = (column[None, :] >= lowest[:, None]) & (column[None, :] <= highest[:, None])
    return inside.astype(jnp.int32)


def block_scale(rng, shape, split, smallest, high):
    def one(dim, shards_of):
        draws = jax.random.uniform(jax.random.fold_in(jax.random.fold_in(rng, 6), dim), (shards_of,), jnp.float32, smallest / len(split), high / len(split))
        return jnp.repeat(jnp.exp(draws), shape[dim] // shards_of).reshape((-1,) + (1,) * (len(shape) - dim - 1))

    gain = one(*split[0])
    for cut in split[1:]:
        gain = gain * one(*cut)
    return gain


def centred(stream_key, shape, width, bound, pieces=(), kind=jnp.bfloat16):
    array = jax.random.normal(stream_key, shape, jnp.float32) * width
    if len(pieces) > 0:
        array = block_scale(stream_key, shape, pieces, -0.22, 0.18) * array
    return jnp.clip(array, min=-bound, max=bound).astype(kind)


def setup_inputs(seed: int = 0) -> dict:
    arg_keys = jax.random.split(jax.random.key(seed), 11)
    gene_act = centred(arg_keys[0], (GENES, D), 1.0, 6.0, ((0, 8),))
    peak_act = centred(arg_keys[1], (PEAKS, D), 1.0, 6.0, ((0, 8),))
    w_query = centred(arg_keys[2], (D, D), D ** -0.5, 0.1875, ((1, 4),))
    w_key = centred(arg_keys[3], (D, D), D ** -0.5, 0.1875, ((1, 4),))
    w_value = centred(arg_keys[4], (D, D), D ** -0.5, 0.1875, ((1, 4),))
    w_out = centred(arg_keys[5], (D, D), D ** -0.5, 0.1875, ((0, 4),))
    head_bias = jnp.clip(-6.0 + 3.0 * jax.random.uniform(arg_keys[6], (HEADS,), jnp.float32) ** block_scale(arg_keys[6], (HEADS,), ((0, 4),), -0.2, 0.2), -6.0, -3.0)
    block_mask = draw_block_mask(jax.random.fold_in(arg_keys[10], 71), 0)
    gene_chrom = draw_gene_chrom(jax.random.fold_in(arg_keys[10], 71), 0)
    peak_chrom = draw_peak_chrom(jax.random.fold_in(arg_keys[10], 71), 0)
    return dict(gene_act=gene_act, peak_act=peak_act, w_query=w_query, w_key=w_key, w_value=w_value, w_out=w_out, head_bias=head_bias, block_mask=block_mask, gene_chrom=gene_chrom, peak_chrom=peak_chrom)


def expand_tiles(tiles, tile_rows):
    rows, cols = tiles.shape
    spread = jnp.broadcast_to(tiles.astype(jnp.float32)[:, None, :, None], (rows, tile_rows, cols, tile_rows))
    return spread.reshape(rows * tile_rows, cols * tile_rows)

def reference(gene_act, peak_act, w_query, w_key, w_value, w_out, head_bias, block_mask, gene_chrom, peak_chrom):
    head_dim = D // HEADS
    queries = jnp.dot(gene_act, w_query, preferred_element_type=jnp.float32).astype(jnp.bfloat16).reshape(GENES, HEADS, head_dim)
    keys_all = jnp.dot(peak_act, w_key, preferred_element_type=jnp.float32).astype(jnp.bfloat16).reshape(PEAKS, HEADS, head_dim)
    values_all = jnp.dot(peak_act, w_value, preferred_element_type=jnp.float32).astype(jnp.bfloat16).reshape(PEAKS, HEADS, head_dim)
    margin = REACH * PEAK_DEV
    keys_pad = jnp.pad(keys_all, ((margin, margin), (0, 0), (0, 0)))
    values_pad = jnp.pad(values_all, ((margin, margin), (0, 0), (0, 0)))
    tile_margin = REACH * (PEAK_DEV // TILE)
    mask_pad = jnp.pad(block_mask, ((0, 0), (tile_margin, tile_margin)))
    tag_pad = jnp.pad(peak_chrom, (margin, margin), constant_values=-1)
    window = (2 * REACH + 1) * PEAK_DEV
    gene_tiles = GENE_DEV // TILE
    window_tiles = window // TILE
    peak_tiles = PEAK_DEV // TILE
    scale = 1.0 / math.sqrt(head_dim)

    def one_block(block):
        start = (block * PEAK_DEV).astype(jnp.int32)
        gene_start = (block * GENE_DEV).astype(jnp.int32)
        query_rows = lax.dynamic_slice_in_dim(queries, gene_start, GENE_DEV, 0)
        key_rows = lax.dynamic_slice_in_dim(keys_pad, start, window, 0)
        value_rows = lax.dynamic_slice_in_dim(values_pad, start, window, 0)
        tiles = lax.dynamic_slice(mask_pad, ((block * gene_tiles).astype(jnp.int32), (block * peak_tiles).astype(jnp.int32)), (gene_tiles, window_tiles))
        gene_tag = lax.dynamic_slice_in_dim(gene_chrom, gene_start, GENE_DEV)
        peak_tag = lax.dynamic_slice_in_dim(tag_pad, start, window)
        allowed = expand_tiles(tiles, TILE) * (gene_tag[:, None] == peak_tag[None, :]).astype(jnp.float32)
        scores = jnp.einsum('ghd,phd->hgp', query_rows.astype(jnp.float32), key_rows.astype(jnp.float32))
        scores = scores * scale + head_bias[:, None, None]
        weights = (jax.nn.sigmoid(scores) * allowed[None]).astype(jnp.bfloat16)
        summed = jnp.einsum('hgp,phd->ghd', weights.astype(jnp.float32), value_rows.astype(jnp.float32))
        return summed.astype(jnp.bfloat16)
    attended = lax.map(one_block, jnp.arange(N_PEAK, dtype=jnp.int32))
    attended = attended.reshape(GENES, D)
    return jnp.dot(attended, w_out, preferred_element_type=jnp.float32).astype(jnp.bfloat16)
```

```python
import functools
import math

import jax
import jax.numpy as jnp
from jax import lax
from jax.experimental import pallas as pl
from jax.experimental.pallas import tpu as pltpu
from jax.sharding import PartitionSpec as P

TILE = 128
REACH = 2
SLOTS = 2 * REACH + 1
CHUNK_TILES = 4
LOG2E = 1.4426950408889634
MESH = pl.DeviceIdType.MESH
VMEM_LIMIT = 48 * 1024 * 1024


def remote(src, dst, send_sem, recv_sem, where):
    return pltpu.make_async_remote_copy(
        src_ref=src,
        dst_ref=dst,
        send_sem=send_sem,
        recv_sem=recv_sem,
        device_id=where,
        device_id_type=MESH,
    )


def places(n):
    me = lax.axis_index("peak")
    odd = lax.rem(me, 2)
    partner = me + 1 - 2 * odd
    ahead = me + 2 - 4 * odd
    behind = me - 2 + 4 * odd
    return me, odd, partner, ahead, behind


def inside(shard, n):
    return (shard >= 0) & (shard < n)


def greet(me, partner, n, gene_peers):
    barrier = pltpu.get_barrier_semaphore()
    pl.semaphore_signal(barrier, inc=1, device_id={"peak": partner}, device_id_type=MESH)
    for far in (me + 2, me - 2):

        @pl.when(inside(far, n))
        def _():
            pl.semaphore_signal(barrier, inc=1, device_id={"peak": far}, device_id_type=MESH)

    for peer in gene_peers:
        pl.semaphore_signal(barrier, inc=1, device_id={"gene": peer}, device_id_type=MESH)
    count = (
        1
        + len(gene_peers)
        + inside(me + 2, n).astype(jnp.int32)
        + inside(me - 2, n).astype(jnp.int32)
    )
    return barrier, count


def exchange_kernel(
    n,
    gn,
    gene_act,
    peak_act,
    w_query,
    w_key,
    w_value,
    w_out,
    q_all,
    keys,
    values,
    wo_all,
    ga,
    pa,
    wq,
    wk,
    wv,
    q_own,
    load_sem,
    local_sem,
    send_sem,
    recv_sem,
    w_send,
    w_recv,
):
    me, odd, partner, ahead, behind = places(n)
    g = lax.axis_index("gene")
    chunks = gene_act.shape[0] // TILE
    piece = peak_act.shape[0] // chunks
    cols = w_out.shape[1] // gn
    pslot = 3 - 2 * odd
    rslot = 1 + 2 * odd
    others = [lax.rem(g + r, gn) for r in range(1, gn)]
    barrier, count = greet(me, partner, n, others)

    loads = [
        pltpu.make_async_copy(src, dst, load_sem.at[i])
        for i, (src, dst) in enumerate(
            ((gene_act, ga), (w_query, wq), (w_key, wk), (w_value, wv))
        )
    ]
    for load in loads:
        load.start()
    peak_loads = [
        pltpu.make_async_copy(
            peak_act.at[pl.ds(c * piece, piece)], pa.at[pl.ds(c * piece, piece)], load_sem.at[4 + c]
        )
        for c in range(chunks)
    ]
    for load in peak_loads:
        load.start()
    loads[0].wait()
    loads[1].wait()
    rows = [pl.ds(c * TILE, TILE) for c in range(chunks)]
    q_own[...] = jnp.dot(ga[...], wq[...], preferred_element_type=jnp.float32).astype(q_own.dtype)
    pl.semaphore_wait(barrier, count)

    def to_partner(c):
        return remote(
            q_own.at[rows[c]],
            q_all.at[rslot, rows[c]],
            send_sem.at[0, c],
            recv_sem.at[rslot, c],
            {"peak": partner},
        )

    def from_partner(c):
        return remote(
            q_own.at[rows[c]],
            q_all.at[pslot, rows[c]],
            send_sem.at[0, c],
            recv_sem.at[pslot, c],
            {"peak": partner},
        )

    def to_far(c, up):
        slot = 0 if up else SLOTS - 1
        return remote(
            q_own.at[rows[c]],
            q_all.at[slot, rows[c]],
            send_sem.at[1 if up else 2, c],
            recv_sem.at[slot, c],
            {"peak": me + 2 if up else me - 2},
        )

    def relayed(c):
        return remote(
            q_all.at[pslot, rows[c]],
            q_all.at[rslot, rows[c]],
            send_sem.at[3, c],
            recv_sem.at[rslot, c],
            {"peak": ahead},
        )

    for c in range(chunks):
        to_partner(c).start()
    for up in (True, False):

        @pl.when(inside(me + 2 if up else me - 2, n))
        def _():
            for c in range(chunks):
                to_far(c, up).start()

    own = pltpu.make_async_copy(q_own, q_all.at[REACH], local_sem.at[0])
    own.start()
    here = pl.ds(pl.multiple_of(g * cols, TILE), cols)
    own_w = pltpu.make_async_copy(w_out.at[:, here], wo_all.at[g], local_sem.at[1])
    own_w.start()
    for r, peer in enumerate(others):
        there = pl.ds(pl.multiple_of(peer * cols, TILE), cols)
        remote(
            w_out.at[:, there], wo_all.at[g], w_send.at[r], w_recv.at[r], {"gene": peer}
        ).start()

    loads[2].wait()
    loads[3].wait()
    for c in range(chunks):
        part = pl.ds(c * piece, piece)
        peak_loads[c].wait()
        keys[part] = jnp.dot(pa[part], wk[...], preferred_element_type=jnp.float32).astype(keys.dtype)
        values[part] = jnp.dot(pa[part], wv[...], preferred_element_type=jnp.float32).astype(
            values.dtype
        )
        from_partner(c).wait_recv()

        @pl.when(inside(ahead, n))
        def _():
            relayed(c).start()

    for c in range(chunks):
        to_partner(c).wait_send()
    for up in (True, False):

        @pl.when(inside(me + 2 if up else me - 2, n))
        def _():
            for c in range(chunks):
                to_far(c, up).wait_send()

        @pl.when(inside(me - 2 if up else me + 2, n))
        def _():
            for c in range(chunks):
                to_far(c, up).wait_recv()

    @pl.when(inside(ahead, n))
    def _():
        for c in range(chunks):
            relayed(c).wait_send()

    @pl.when(inside(behind, n))
    def _():
        for c in range(chunks):
            relayed(c).wait_recv()

    own.wait()
    own_w.wait()
    for r, peer in enumerate(others):
        there = pl.ds(pl.multiple_of(peer * cols, TILE), cols)
        source = lax.rem(g + gn - 1 - r, gn)
        copy = remote(
            w_out.at[:, there], wo_all.at[source], w_send.at[r], w_recv.at[r], {"gene": peer}
        )
        copy.wait_send()
        copy.wait_recv()


def attend_kernel(
    n, codes, head_bias, gene_chrom, peak_chrom, q_all, keys, values, parts, total, where
):
    me = where[0]
    gene_tiles = q_all.shape[1] // TILE
    peak_rows = keys.shape[0]
    peak_tiles = peak_rows // TILE
    chunk = CHUNK_TILES * TILE
    chunks = peak_rows // chunk
    heads = head_bias.shape[0]
    dim = keys.shape[1] // heads
    factor = -LOG2E / math.sqrt(dim)

    def one_tile(step, carry):
        slot = step // gene_tiles
        tile = step % gene_tiles
        source = me + slot - REACH

        @pl.when(inside(source, n))
        def _():
            gene_tile = source * gene_tiles + tile
            rows = pl.ds(pl.multiple_of(tile * TILE, TILE), TILE)
            total[...] = jnp.zeros_like(total)

            def one_chunk(c, carry):
                code = codes[gene_tile, me * chunks + c]

                @pl.when(code != 0)
                def _():
                    row = gene_chrom[pl.ds(gene_tile, 1), :]
                    gene_tag = jnp.transpose(jnp.broadcast_to(row, (TILE, TILE)))
                    allowed = []
                    for t in range(CHUNK_TILES):
                        tags = peak_chrom[pl.ds(me * peak_tiles + c * CHUNK_TILES + t, 1), :]
                        tags = jnp.where((code >> t) & 1 == 1, tags, -1)
                        allowed.append(gene_tag == tags)
                    allowed = jnp.concatenate(allowed, axis=1)
                    at = pl.ds(pl.multiple_of(c * chunk, chunk), chunk)
                    for h in range(heads):
                        head = pl.ds(h * dim, dim)
                        scores = lax.dot_general(
                            q_all[slot, rows, head],
                            keys[at, head],
                            (((1,), (1,)), ((), ())),
                            preferred_element_type=jnp.float32,
                        )
                        grown = jnp.exp2(scores * factor - head_bias[h] * LOG2E)
                        weights = pl.reciprocal(1.0 + grown, approx=True)
                        weights = jnp.where(allowed, weights, 0.0).astype(jnp.bfloat16)
                        total[:, head] += jnp.dot(
                            weights, values[at, head], preferred_element_type=jnp.float32
                        )

                return carry

            lax.fori_loop(0, chunks, one_chunk, 0)
            parts[slot, rows] = total[...].astype(parts.dtype)

        return carry

    lax.fori_loop(0, SLOTS * gene_tiles, one_tile, 0)


def mix_kernel(
    n,
    gn,
    parts,
    wo_all,
    mixed,
    from_up,
    from_down,
    diagonal,
    joined,
    summed,
    attended,
    far_send,
    far_recv,
    near_send,
    near_recv,
    gene_send,
    gene_recv,
):
    me, odd, partner, ahead, behind = places(n)
    g = lax.axis_index("gene")
    chunks = parts.shape[1] // TILE
    pslot = 3 - 2 * odd
    rslot = 1 + 2 * odd
    core = g + 1 - 2 * lax.rem(g, 2)
    across = [lax.rem(g + 2 * r, gn) for r in range(1, gn // 2)]
    barrier, count = greet(me, partner, n, [core] + across)
    rows = [pl.ds(c * TILE, TILE) for c in range(chunks)]
    pl.semaphore_wait(barrier, count)

    def diag(c):
        return remote(
            parts.at[rslot, rows[c]],
            diagonal.at[rows[c]],
            near_send.at[0, c],
            near_recv.at[0, c],
            {"peak": behind},
        )

    def join(c):
        return remote(
            joined.at[rows[c]],
            summed.at[rows[c]],
            near_send.at[1, c],
            near_recv.at[1, c],
            {"peak": partner},
        )

    def far(c, up):
        return remote(
            parts.at[SLOTS - 1 if up else 0, rows[c]],
            (from_down if up else from_up).at[rows[c]],
            far_send.at[0 if up else 1, c],
            far_recv.at[0 if up else 1, c],
            {"peak": me + 2 if up else me - 2},
        )

    @pl.when(inside(behind, n))
    def _():
        for c in range(chunks):
            diag(c).start()

    for up in (True, False):

        @pl.when(inside(me + 2 if up else me - 2, n))
        def _():
            for c in range(chunks):
                far(c, up).start()

    for c in range(chunks):

        @pl.when(inside(ahead, n))
        def _():
            diag(c).wait_recv()
            joined[rows[c]] = (
                parts[pslot, rows[c]].astype(jnp.float32) + diagonal[rows[c]].astype(jnp.float32)
            ).astype(joined.dtype)

        @pl.when(jnp.logical_not(inside(ahead, n)))
        def _():
            joined[rows[c]] = parts[pslot, rows[c]]

        join(c).start()

    def gather(c, block, peer, lane):
        return remote(
            attended.at[block, rows[c]],
            attended.at[block, rows[c]],
            gene_send.at[lane, c],
            gene_recv.at[block, c],
            {"gene": peer},
        )

    def finish(c):
        for r, peer in enumerate(across):
            gather(c, peer, peer, 0).wait_recv()
            gather(c, peer, core, len(across) + 1 + r).start()

    def product(c):
        gather(c, core, core, 0).wait_recv()
        for peer in across:
            gather(c, peer + 1 - 2 * lax.rem(peer, 2), core, 0).wait_recv()
        out = jnp.dot(attended[0, rows[c]], wo_all[0], preferred_element_type=jnp.float32)
        for block in range(1, gn):
            out += jnp.dot(
                attended[block, rows[c]], wo_all[block], preferred_element_type=jnp.float32
            )
        mixed[rows[c]] = out.astype(mixed.dtype)

    for c in range(chunks):
        join(c).wait_recv()
        for up in (True, False):

            @pl.when(inside(me - 2 if up else me + 2, n))
            def _():
                far(c, up).wait_recv()

        total = parts[REACH, rows[c]].astype(jnp.float32) + summed[rows[c]].astype(jnp.float32)
        low = jnp.where(inside(me - 2, n), from_down[rows[c]].astype(jnp.float32), 0.0)
        high = jnp.where(inside(me + 2, n), from_up[rows[c]].astype(jnp.float32), 0.0)
        attended[g, rows[c]] = (total + low + high).astype(attended.dtype)
        gather(c, g, core, 0).start()
        for r, peer in enumerate(across):
            gather(c, g, peer, 1 + r).start()
        if c >= 1:
            finish(c - 1)
    finish(chunks - 1)
    for c in range(chunks):
        product(c)

    for c in range(chunks):
        join(c).wait_send()
        for lane in range(1 + 2 * len(across)):
            gather(c, g, core, lane).wait_send()
    for up in (True, False):

        @pl.when(inside(me + 2 if up else me - 2, n))
        def _():
            for c in range(chunks):
                far(c, up).wait_send()

    @pl.when(inside(behind, n))
    def _():
        for c in range(chunks):
            diag(c).wait_send()


def on_device(
    gene_act,
    peak_act,
    w_query,
    w_key,
    w_value,
    w_out,
    head_bias,
    block_mask,
    gene_chrom,
    peak_chrom,
):
    n, gn = lax.axis_size("peak"), lax.axis_size("gene")
    gene_rows, peak_rows = gene_act.shape[0], peak_act.shape[0]
    width = w_query.shape[1]
    cols = w_out.shape[1] // gn
    chunks = gene_rows // TILE
    dtype = gene_act.dtype
    anywhere = pl.BlockSpec(memory_space=pl.ANY)
    in_vmem = pl.BlockSpec(memory_space=pltpu.VMEM)
    in_smem = pl.BlockSpec(memory_space=pltpu.SMEM)

    q_all, keys, values, wo_all = pl.pallas_call(
        functools.partial(exchange_kernel, n, gn),
        out_shape=(
            jax.ShapeDtypeStruct((SLOTS, gene_rows, width), dtype),
            jax.ShapeDtypeStruct((peak_rows, width), dtype),
            jax.ShapeDtypeStruct((peak_rows, width), dtype),
            jax.ShapeDtypeStruct((gn, w_out.shape[0], cols), dtype),
        ),
        in_specs=[anywhere] * 6,
        out_specs=(anywhere, in_vmem, in_vmem, anywhere),
        scratch_shapes=[
            pltpu.VMEM(gene_act.shape, dtype),
            pltpu.VMEM(peak_act.shape, dtype),
            pltpu.VMEM(w_query.shape, dtype),
            pltpu.VMEM(w_key.shape, dtype),
            pltpu.VMEM(w_value.shape, dtype),
            pltpu.VMEM((gene_rows, width), dtype),
            pltpu.SemaphoreType.DMA((4 + chunks,)),
            pltpu.SemaphoreType.DMA((2,)),
            pltpu.SemaphoreType.DMA((4, chunks)),
            pltpu.SemaphoreType.DMA((SLOTS, chunks)),
            pltpu.SemaphoreType.DMA((gn - 1,)),
            pltpu.SemaphoreType.DMA((gn - 1,)),
        ],
        compiler_params=pltpu.CompilerParams(
            collective_id=0, has_side_effects=True, vmem_limit_bytes=VMEM_LIMIT
        ),
    )(gene_act, peak_act, w_query, w_key, w_value, w_out)

    gene_tags = gene_chrom.reshape(-1, TILE)
    peak_tags = peak_chrom.reshape(-1, TILE)
    overlap = (
        (block_mask == 1)
        & (gene_tags[:, :1] <= peak_tags[:, -1][None, :])
        & (peak_tags[:, 0][None, :] <= gene_tags[:, -1:])
    )
    bits = overlap.astype(jnp.int32).reshape(overlap.shape[0], -1, CHUNK_TILES)
    codes = jnp.sum(bits << jnp.arange(CHUNK_TILES, dtype=jnp.int32), axis=2)
    where = lax.axis_index("peak").astype(jnp.int32).reshape(1)

    def attend(where, codes, bias, genes, peaks, q, k, v, parts, total):
        attend_kernel(n, codes, bias, genes, peaks, q, k, v, parts, total, where)

    parts = pl.pallas_call(
        attend,
        out_shape=jax.ShapeDtypeStruct((SLOTS, gene_rows, width), dtype),
        in_specs=[in_smem] * 3 + [in_vmem] * 5,
        out_specs=in_vmem,
        scratch_shapes=[pltpu.VMEM((TILE, width), jnp.float32)],
        compiler_params=pltpu.CompilerParams(vmem_limit_bytes=VMEM_LIMIT),
    )(where, codes, head_bias, gene_tags, peak_tags, q_all, keys, values)

    return pl.pallas_call(
        functools.partial(mix_kernel, n, gn),
        out_shape=jax.ShapeDtypeStruct((gene_rows, cols), dtype),
        in_specs=[in_vmem, in_vmem],
        out_specs=in_vmem,
        scratch_shapes=[pltpu.VMEM((gene_rows, width), dtype)] * 5
        + [
            pltpu.VMEM((gn, gene_rows, width), dtype),
            pltpu.SemaphoreType.DMA((2, chunks)),
            pltpu.SemaphoreType.DMA((2, chunks)),
            pltpu.SemaphoreType.DMA((2, chunks)),
            pltpu.SemaphoreType.DMA((2, chunks)),
            pltpu.SemaphoreType.DMA((gn, chunks)),
            pltpu.SemaphoreType.DMA((gn, chunks)),
        ],
        compiler_params=pltpu.CompilerParams(
            collective_id=1, has_side_effects=True, vmem_limit_bytes=VMEM_LIMIT
        ),
    )(parts, wo_all)


def solution(mesh):
    placed = (
        P("peak", None),
        P("peak", None),
        P(None, "gene"),
        P(None, "gene"),
        P(None, "gene"),
        P("gene", None),
        P("gene"),
        P(),
        P(),
        P(),
    )
    return jax.shard_map(
        on_device, mesh=mesh, in_specs=placed, out_specs=P("peak", "gene"), check_vma=False
    )
```

```python
import functools
import math

import jax
import jax.numpy as jnp
from jax import lax
from jax.experimental import pallas as pl
from jax.experimental.pallas import tpu as pltpu
from jax.sharding import PartitionSpec as P

TILE = 128
REACH = 2
CHUNK_TILES = 4
LOG2E = 1.4426950408889634
MESH = pl.DeviceIdType.MESH
VMEM_LIMIT = 48 * 1024 * 1024


def remote(src, dst, send_sem, recv_sem, where):
    return pltpu.make_async_remote_copy(
        src_ref=src,
        dst_ref=dst,
        send_sem=send_sem,
        recv_sem=recv_sem,
        device_id=where,
        device_id_type=MESH,
    )


def places(n):
    me = lax.axis_index("peak")
    odd = lax.rem(me, 2)
    partner = me + 1 - 2 * odd
    ahead = me + 2 - 4 * odd
    behind = me - 2 + 4 * odd
    return me, odd, partner, ahead, behind


def inside(shard, n):
    return (shard >= 0) & (shard < n)


def greet(me, partner, n, gene_peers):
    barrier = pltpu.get_barrier_semaphore()
    pl.semaphore_signal(barrier, inc=1, device_id={"peak": partner}, device_id_type=MESH)
    for far in (me + 2, me - 2):

        @pl.when(inside(far, n))
        def _():
            pl.semaphore_signal(barrier, inc=1, device_id={"peak": far}, device_id_type=MESH)

    for peer in gene_peers:
        pl.semaphore_signal(barrier, inc=1, device_id={"gene": peer}, device_id_type=MESH)
    count = (
        1
        + len(gene_peers)
        + inside(me + 2, n).astype(jnp.int32)
        + inside(me - 2, n).astype(jnp.int32)
    )
    return barrier, count


def exchange_kernel(
    n,
    gn,
    reach,
    gene_act,
    peak_act,
    w_query,
    w_key,
    w_value,
    w_out,
    q_all,
    keys,
    values,
    wo_all,
    ga,
    pa,
    wq,
    wk,
    wv,
    q_own,
    load_sem,
    local_sem,
    send_sem,
    recv_sem,
    w_send,
    w_recv,
):
    me, odd, partner, ahead, behind = places(n)
    g = lax.axis_index("gene")
    chunks = gene_act.shape[0] // TILE
    piece = peak_act.shape[0] // chunks
    cols = w_out.shape[1] // gn
    pslot = reach + 1 - 2 * odd
    rslot = reach - 1 + 2 * odd
    ways = (True, False) if reach > 1 else ()
    others = [lax.rem(g + r, gn) for r in range(1, gn)]
    barrier, count = greet(me, partner, n, others)

    loads = [
        pltpu.make_async_copy(src, dst, load_sem.at[i])
        for i, (src, dst) in enumerate(
            ((gene_act, ga), (w_query, wq), (w_key, wk), (w_value, wv))
        )
    ]
    for load in loads:
        load.start()
    peak_loads = [
        pltpu.make_async_copy(
            peak_act.at[pl.ds(c * piece, piece)], pa.at[pl.ds(c * piece, piece)], load_sem.at[4 + c]
        )
        for c in range(chunks)
    ]
    for load in peak_loads:
        load.start()
    loads[0].wait()
    loads[1].wait()
    rows = [pl.ds(c * TILE, TILE) for c in range(chunks)]
    q_own[...] = jnp.dot(ga[...], wq[...], preferred_element_type=jnp.float32).astype(q_own.dtype)
    pl.semaphore_wait(barrier, count)

    def to_partner(c):
        return remote(
            q_own.at[rows[c]],
            q_all.at[rslot, rows[c]],
            send_sem.at[0, c],
            recv_sem.at[rslot, c],
            {"peak": partner},
        )

    def from_partner(c):
        return remote(
            q_own.at[rows[c]],
            q_all.at[pslot, rows[c]],
            send_sem.at[0, c],
            recv_sem.at[pslot, c],
            {"peak": partner},
        )

    def to_far(c, up):
        slot = 0 if up else 2 * reach
        return remote(
            q_own.at[rows[c]],
            q_all.at[slot, rows[c]],
            send_sem.at[1 if up else 2, c],
            recv_sem.at[slot, c],
            {"peak": me + 2 if up else me - 2},
        )

    def relayed(c):
        return remote(
            q_all.at[pslot, rows[c]],
            q_all.at[rslot, rows[c]],
            send_sem.at[3, c],
            recv_sem.at[rslot, c],
            {"peak": ahead},
        )

    for c in range(chunks):
        to_partner(c).start()
    for up in ways:

        @pl.when(inside(me + 2 if up else me - 2, n))
        def _():
            for c in range(chunks):
                to_far(c, up).start()

    own = pltpu.make_async_copy(q_own, q_all.at[reach], local_sem.at[0])
    own.start()
    here = pl.ds(pl.multiple_of(g * cols, TILE), cols)
    own_w = pltpu.make_async_copy(w_out.at[:, here], wo_all.at[g], local_sem.at[1])
    own_w.start()
    for r, peer in enumerate(others):
        there = pl.ds(pl.multiple_of(peer * cols, TILE), cols)
        remote(
            w_out.at[:, there], wo_all.at[g], w_send.at[r], w_recv.at[r], {"gene": peer}
        ).start()

    loads[2].wait()
    loads[3].wait()
    for c in range(chunks):
        part = pl.ds(c * piece, piece)
        peak_loads[c].wait()
        keys[part] = jnp.dot(pa[part], wk[...], preferred_element_type=jnp.float32).astype(keys.dtype)
        values[part] = jnp.dot(pa[part], wv[...], preferred_element_type=jnp.float32).astype(
            values.dtype
        )
        from_partner(c).wait_recv()

        @pl.when(inside(ahead, n))
        def _():
            relayed(c).start()

    for c in range(chunks):
        to_partner(c).wait_send()
    for up in ways:

        @pl.when(inside(me + 2 if up else me - 2, n))
        def _():
            for c in range(chunks):
                to_far(c, up).wait_send()

        @pl.when(inside(me - 2 if up else me + 2, n))
        def _():
            for c in range(chunks):
                to_far(c, up).wait_recv()

    @pl.when(inside(ahead, n))
    def _():
        for c in range(chunks):
            relayed(c).wait_send()

    @pl.when(inside(behind, n))
    def _():
        for c in range(chunks):
            relayed(c).wait_recv()

    own.wait()
    own_w.wait()
    for r, peer in enumerate(others):
        there = pl.ds(pl.multiple_of(peer * cols, TILE), cols)
        source = lax.rem(g + gn - 1 - r, gn)
        copy = remote(
            w_out.at[:, there], wo_all.at[source], w_send.at[r], w_recv.at[r], {"gene": peer}
        )
        copy.wait_send()
        copy.wait_recv()


def attend_kernel(
    n, reach, codes, head_bias, gene_chrom, peak_chrom, q_all, keys, values, parts, total, where
):
    me = where[0]
    gene_tiles = q_all.shape[1] // TILE
    peak_rows = keys.shape[0]
    peak_tiles = peak_rows // TILE
    chunk = CHUNK_TILES * TILE
    chunks = peak_rows // chunk
    heads = head_bias.shape[0]
    dim = keys.shape[1] // heads
    factor = -LOG2E / math.sqrt(dim)

    def one_tile(step, carry):
        slot = step // gene_tiles
        tile = step % gene_tiles
        source = me + slot - reach

        @pl.when(inside(source, n))
        def _():
            gene_tile = source * gene_tiles + tile
            rows = pl.ds(pl.multiple_of(tile * TILE, TILE), TILE)
            total[...] = jnp.zeros_like(total)

            def one_chunk(c, carry):
                code = codes[gene_tile, me * chunks + c]

                @pl.when(code != 0)
                def _():
                    row = gene_chrom[pl.ds(gene_tile, 1), :]
                    gene_tag = jnp.transpose(jnp.broadcast_to(row, (TILE, TILE)))
                    allowed = []
                    for t in range(CHUNK_TILES):
                        tags = peak_chrom[pl.ds(me * peak_tiles + c * CHUNK_TILES + t, 1), :]
                        tags = jnp.where((code >> t) & 1 == 1, tags, -1)
                        allowed.append(gene_tag == tags)
                    allowed = jnp.concatenate(allowed, axis=1)
                    at = pl.ds(pl.multiple_of(c * chunk, chunk), chunk)
                    for h in range(heads):
                        head = pl.ds(h * dim, dim)
                        scores = lax.dot_general(
                            q_all[slot, rows, head],
                            keys[at, head],
                            (((1,), (1,)), ((), ())),
                            preferred_element_type=jnp.float32,
                        )
                        grown = jnp.exp2(scores * factor - head_bias[h] * LOG2E)
                        weights = pl.reciprocal(1.0 + grown, approx=True)
                        weights = jnp.where(allowed, weights, 0.0).astype(jnp.bfloat16)
                        total[:, head] += jnp.dot(
                            weights, values[at, head], preferred_element_type=jnp.float32
                        )

                return carry

            lax.fori_loop(0, chunks, one_chunk, 0)
            parts[slot, rows] = total[...].astype(parts.dtype)

        return carry

    lax.fori_loop(0, (2 * reach + 1) * gene_tiles, one_tile, 0)


def mix_kernel(
    n,
    gn,
    reach,
    parts,
    wo_all,
    mixed,
    from_up,
    from_down,
    diagonal,
    joined,
    summed,
    attended,
    far_send,
    far_recv,
    near_send,
    near_recv,
    gene_send,
    gene_recv,
):
    me, odd, partner, ahead, behind = places(n)
    g = lax.axis_index("gene")
    chunks = parts.shape[1] // TILE
    pslot = reach + 1 - 2 * odd
    rslot = reach - 1 + 2 * odd
    ways = (True, False) if reach > 1 else ()
    core = g + 1 - 2 * lax.rem(g, 2)
    across = [lax.rem(g + 2 * r, gn) for r in range(1, gn // 2)]
    barrier, count = greet(me, partner, n, [core] + across)
    rows = [pl.ds(c * TILE, TILE) for c in range(chunks)]
    pl.semaphore_wait(barrier, count)

    def diag(c):
        return remote(
            parts.at[rslot, rows[c]],
            diagonal.at[rows[c]],
            near_send.at[0, c],
            near_recv.at[0, c],
            {"peak": behind},
        )

    def join(c):
        return remote(
            joined.at[rows[c]],
            summed.at[rows[c]],
            near_send.at[1, c],
            near_recv.at[1, c],
            {"peak": partner},
        )

    def far(c, up):
        return remote(
            parts.at[2 * reach if up else 0, rows[c]],
            (from_down if up else from_up).at[rows[c]],
            far_send.at[0 if up else 1, c],
            far_recv.at[0 if up else 1, c],
            {"peak": me + 2 if up else me - 2},
        )

    @pl.when(inside(behind, n))
    def _():
        for c in range(chunks):
            diag(c).start()

    for up in ways:

        @pl.when(inside(me + 2 if up else me - 2, n))
        def _():
            for c in range(chunks):
                far(c, up).start()

    for c in range(chunks):

        @pl.when(inside(ahead, n))
        def _():
            diag(c).wait_recv()
            joined[rows[c]] = (
                parts[pslot, rows[c]].astype(jnp.float32) + diagonal[rows[c]].astype(jnp.float32)
            ).astype(joined.dtype)

        @pl.when(jnp.logical_not(inside(ahead, n)))
        def _():
            joined[rows[c]] = parts[pslot, rows[c]]

        join(c).start()

    def gather(c, block, peer, lane):
        return remote(
            attended.at[block, rows[c]],
            attended.at[block, rows[c]],
            gene_send.at[lane, c],
            gene_recv.at[block, c],
            {"gene": peer},
        )

    def finish(c):
        for r, peer in enumerate(across):
            gather(c, peer, peer, 0).wait_recv()
            gather(c, peer, core, len(across) + 1 + r).start()

    def product(c):
        gather(c, core, core, 0).wait_recv()
        for peer in across:
            gather(c, peer + 1 - 2 * lax.rem(peer, 2), core, 0).wait_recv()
        out = jnp.dot(attended[0, rows[c]], wo_all[0], preferred_element_type=jnp.float32)
        for block in range(1, gn):
            out += jnp.dot(
                attended[block, rows[c]], wo_all[block], preferred_element_type=jnp.float32
            )
        mixed[rows[c]] = out.astype(mixed.dtype)

    for c in range(chunks):
        join(c).wait_recv()
        for up in ways:

            @pl.when(inside(me - 2 if up else me + 2, n))
            def _():
                far(c, up).wait_recv()

        total = parts[reach, rows[c]].astype(jnp.float32) + summed[rows[c]].astype(jnp.float32)
        if reach > 1:
            low = jnp.where(inside(me - 2, n), from_down[rows[c]].astype(jnp.float32), 0.0)
            high = jnp.where(inside(me + 2, n), from_up[rows[c]].astype(jnp.float32), 0.0)
            total = total + low + high
        attended[g, rows[c]] = total.astype(attended.dtype)
        gather(c, g, core, 0).start()
        for r, peer in enumerate(across):
            gather(c, g, peer, 1 + r).start()
        if c >= 1:
            finish(c - 1)
    finish(chunks - 1)
    for c in range(chunks):
        product(c)

    for c in range(chunks):
        join(c).wait_send()
        for lane in range(1 + 2 * len(across)):
            gather(c, g, core, lane).wait_send()
    for up in ways:

        @pl.when(inside(me + 2 if up else me - 2, n))
        def _():
            for c in range(chunks):
                far(c, up).wait_send()

    @pl.when(inside(behind, n))
    def _():
        for c in range(chunks):
            diag(c).wait_send()


def plan_kernel(gene_tiles, peak_tiles, block_mask, gene_tags, peak_tags, codes, far):
    rows, cols = block_mask.shape
    first = jnp.transpose(peak_tags[...])[:1, :]
    last = jnp.transpose(peak_tags[...])[TILE - 1 :, :]
    live = (
        (block_mask[...] == 1)
        & (gene_tags[:, :1] <= last)
        & (first <= gene_tags[:, TILE - 1 :])
    ).astype(jnp.float32)
    tile = lax.broadcasted_iota(jnp.int32, (cols, codes.shape[1]), 0)
    chunk = lax.broadcasted_iota(jnp.int32, (cols, codes.shape[1]), 1)
    bit = jnp.left_shift(1, lax.rem(tile, CHUNK_TILES))
    spread = jnp.where(lax.div(tile, CHUNK_TILES) == chunk, bit, 0).astype(jnp.float32)
    codes[...] = jnp.dot(live, spread, preferred_element_type=jnp.float32).astype(jnp.int32)
    gene_shard = lax.div(lax.broadcasted_iota(jnp.int32, (rows, cols), 0), gene_tiles)
    peak_shard = lax.div(lax.broadcasted_iota(jnp.int32, (rows, cols), 1), peak_tiles)
    apart = jnp.abs(gene_shard - peak_shard) > 1
    far[0, 0] = (jnp.sum(jnp.where(apart, live, 0.0)) > 0.5).astype(jnp.int32)


def layer(
    reach, n, gn, gene_act, peak_act, w_query, w_key, w_value, w_out, head_bias, where, codes,
    gene_tags, peak_tags,
):
    gene_rows, peak_rows = gene_act.shape[0], peak_act.shape[0]
    width = w_query.shape[1]
    cols = w_out.shape[1] // gn
    chunks = gene_rows // TILE
    slots = 2 * reach + 1
    dtype = gene_act.dtype
    in_hbm = pl.BlockSpec(memory_space=pltpu.HBM)
    in_vmem = pl.BlockSpec(memory_space=pltpu.VMEM)
    in_smem = pl.BlockSpec(memory_space=pltpu.SMEM)

    q_all, keys, values, wo_all = pl.pallas_call(
        functools.partial(exchange_kernel, n, gn, reach),
        out_shape=(
            jax.ShapeDtypeStruct((slots, gene_rows, width), dtype),
            jax.ShapeDtypeStruct((peak_rows, width), dtype),
            jax.ShapeDtypeStruct((peak_rows, width), dtype),
            jax.ShapeDtypeStruct((gn, w_out.shape[0], cols), dtype),
        ),
        in_specs=[in_hbm] * 6,
        out_specs=(in_vmem,) * 4,
        scratch_shapes=[
            pltpu.VMEM(gene_act.shape, dtype),
            pltpu.VMEM(peak_act.shape, dtype),
            pltpu.VMEM(w_query.shape, dtype),
            pltpu.VMEM(w_key.shape, dtype),
            pltpu.VMEM(w_value.shape, dtype),
            pltpu.VMEM((gene_rows, width), dtype),
            pltpu.SemaphoreType.DMA((4 + chunks,)),
            pltpu.SemaphoreType.DMA((2,)),
            pltpu.SemaphoreType.DMA((4, chunks)),
            pltpu.SemaphoreType.DMA((slots, chunks)),
            pltpu.SemaphoreType.DMA((gn - 1,)),
            pltpu.SemaphoreType.DMA((gn - 1,)),
        ],
        compiler_params=pltpu.CompilerParams(
            collective_id=2 * reach, has_side_effects=True, vmem_limit_bytes=VMEM_LIMIT
        ),
    )(gene_act, peak_act, w_query, w_key, w_value, w_out)

    def attend(where, codes, bias, genes, peaks, q, k, v, parts, total):
        attend_kernel(n, reach, codes, bias, genes, peaks, q, k, v, parts, total, where)

    parts = pl.pallas_call(
        attend,
        out_shape=jax.ShapeDtypeStruct((slots, gene_rows, width), dtype),
        in_specs=[in_smem] * 3 + [in_vmem] * 5,
        out_specs=in_vmem,
        scratch_shapes=[pltpu.VMEM((TILE, width), jnp.float32)],
        compiler_params=pltpu.CompilerParams(vmem_limit_bytes=VMEM_LIMIT),
    )(where, codes, head_bias, gene_tags, peak_tags, q_all, keys, values)

    return pl.pallas_call(
        functools.partial(mix_kernel, n, gn, reach),
        out_shape=jax.ShapeDtypeStruct((gene_rows, cols), dtype),
        in_specs=[in_vmem, in_vmem],
        out_specs=in_vmem,
        scratch_shapes=[pltpu.VMEM((gene_rows, width), dtype)] * 5
        + [
            pltpu.VMEM((gn, gene_rows, width), dtype),
            pltpu.SemaphoreType.DMA((2, chunks)),
            pltpu.SemaphoreType.DMA((2, chunks)),
            pltpu.SemaphoreType.DMA((2, chunks)),
            pltpu.SemaphoreType.DMA((2, chunks)),
            pltpu.SemaphoreType.DMA((gn, chunks)),
            pltpu.SemaphoreType.DMA((gn, chunks)),
        ],
        compiler_params=pltpu.CompilerParams(
            collective_id=2 * reach + 1, has_side_effects=True, vmem_limit_bytes=VMEM_LIMIT
        ),
    )(parts, wo_all)


def on_device(
    gene_act,
    peak_act,
    w_query,
    w_key,
    w_value,
    w_out,
    head_bias,
    block_mask,
    gene_chrom,
    peak_chrom,
):
    n, gn = lax.axis_size("peak"), lax.axis_size("gene")
    in_vmem = pl.BlockSpec(memory_space=pltpu.VMEM)
    gene_tags = gene_chrom.reshape(-1, TILE)
    peak_tags = peak_chrom.reshape(-1, TILE)
    rows, cols = block_mask.shape
    code_cols = -(-(cols // CHUNK_TILES) // TILE) * TILE
    codes, far = pl.pallas_call(
        functools.partial(plan_kernel, rows // n, cols // n),
        out_shape=(
            jax.ShapeDtypeStruct((rows, code_cols), jnp.int32),
            jax.ShapeDtypeStruct((1, 1), jnp.int32),
        ),
        in_specs=[in_vmem] * 3,
        out_specs=(in_vmem, pl.BlockSpec(memory_space=pltpu.SMEM)),
        compiler_params=pltpu.CompilerParams(vmem_limit_bytes=VMEM_LIMIT),
    )(block_mask, gene_tags, peak_tags)
    where = lax.axis_index("peak").astype(jnp.int32).reshape(1)
    operands = (
        gene_act, peak_act, w_query, w_key, w_value, w_out, head_bias, where, codes, gene_tags,
        peak_tags,
    )
    return lax.cond(
        far[0, 0] > 0,
        functools.partial(layer, REACH, n, gn),
        functools.partial(layer, 1, n, gn),
        *operands,
    )


def solution(mesh):
    placed = (
        P("peak", None),
        P("peak", None),
        P(None, "gene"),
        P(None, "gene"),
        P(None, "gene"),
        P("gene", None),
        P("gene"),
        P(),
        P(),
        P(),
    )
    return jax.shard_map(
        on_device, mesh=mesh, in_specs=placed, out_specs=P("peak", "gene"), check_vma=False
    )
```

```python
import functools
import math

import jax
import jax.numpy as jnp
from jax import lax
from jax.experimental import pallas as pl
from jax.experimental.pallas import tpu as pltpu
from jax.sharding import PartitionSpec as P

TILE = 128
REACH = 2
CHUNK_TILES = 4
LOG2E = 1.4426950408889634
MESH = pl.DeviceIdType.MESH
VMEM_LIMIT = 48 * 1024 * 1024


def remote(src, dst, send_sem, recv_sem, where):
    return pltpu.make_async_remote_copy(
        src_ref=src,
        dst_ref=dst,
        send_sem=send_sem,
        recv_sem=recv_sem,
        device_id=where,
        device_id_type=MESH,
    )


def places(n):
    me = lax.axis_index("peak")
    odd = lax.rem(me, 2)
    partner = me + 1 - 2 * odd
    ahead = me + 2 - 4 * odd
    behind = me - 2 + 4 * odd
    return me, odd, partner, ahead, behind


def inside(shard, n):
    return (shard >= 0) & (shard < n)


def greet(me, partner, n, gene_peers):
    barrier = pltpu.get_barrier_semaphore()
    pl.semaphore_signal(barrier, inc=1, device_id={"peak": partner}, device_id_type=MESH)
    for far in (me + 2, me - 2):

        @pl.when(inside(far, n))
        def _():
            pl.semaphore_signal(barrier, inc=1, device_id={"peak": far}, device_id_type=MESH)

    for peer in gene_peers:
        pl.semaphore_signal(barrier, inc=1, device_id={"gene": peer}, device_id_type=MESH)
    count = (
        1
        + len(gene_peers)
        + inside(me + 2, n).astype(jnp.int32)
        + inside(me - 2, n).astype(jnp.int32)
    )
    return barrier, count


def score(queries, keys):
    return lax.dot_general(
        queries, keys, (((1,), (1,)), ((), ())), preferred_element_type=jnp.float32
    )


def gate(scores, bias, dim):
    grown = jnp.exp2(scores * (-LOG2E / math.sqrt(dim)) - bias * LOG2E)
    return pl.reciprocal(1.0 + grown, approx=True)


def allowed_pairs(gene_tags, peak_tags, gene_tile, chunk, code):
    row = gene_tags[pl.ds(gene_tile, 1), :]
    gene_tag = jnp.transpose(jnp.broadcast_to(row, (TILE, TILE)))
    allowed = []
    for t in range(CHUNK_TILES):
        tags = peak_tags[pl.ds(chunk * CHUNK_TILES + t, 1), :]
        tags = jnp.where((code >> t) & 1 == 1, tags, -1)
        allowed.append(gene_tag == tags)
    return jnp.concatenate(allowed, axis=1)


def exchange_kernel(
    n,
    gn,
    reach,
    gene_act,
    peak_act,
    w_query,
    w_key,
    w_value,
    w_out,
    head_bias,
    codes,
    gene_tags,
    peak_tags,
    q_all,
    keys,
    values,
    wo_all,
    own_part,
    ga,
    pa,
    wq,
    wk,
    wv,
    q_own,
    load_sem,
    local_sem,
    send_sem,
    recv_sem,
    w_send,
    w_recv,
):
    me, odd, partner, ahead, behind = places(n)
    g = lax.axis_index("gene")
    chunks = gene_act.shape[0] // TILE
    piece = peak_act.shape[0] // chunks
    cols = w_out.shape[1] // gn
    pslot = reach + 1 - 2 * odd
    rslot = reach - 1 + 2 * odd
    ways = (True, False) if reach > 1 else ()
    others = [lax.rem(g + r, gn) for r in range(1, gn)]
    barrier, count = greet(me, partner, n, others)

    loads = [
        pltpu.make_async_copy(src, dst, load_sem.at[i])
        for i, (src, dst) in enumerate(
            ((gene_act, ga), (w_query, wq), (w_key, wk), (w_value, wv))
        )
    ]
    for load in loads:
        load.start()
    peak_loads = [
        pltpu.make_async_copy(
            peak_act.at[pl.ds(c * piece, piece)], pa.at[pl.ds(c * piece, piece)], load_sem.at[4 + c]
        )
        for c in range(chunks)
    ]
    for load in peak_loads:
        load.start()
    loads[0].wait()
    loads[1].wait()
    rows = [pl.ds(c * TILE, TILE) for c in range(chunks)]
    q_own[...] = jnp.dot(ga[...], wq[...], preferred_element_type=jnp.float32).astype(q_own.dtype)
    pl.semaphore_wait(barrier, count)

    def to_partner(c):
        return remote(
            q_own.at[rows[c]],
            q_all.at[rslot, rows[c]],
            send_sem.at[0, c],
            recv_sem.at[rslot, c],
            {"peak": partner},
        )

    def from_partner(c):
        return remote(
            q_own.at[rows[c]],
            q_all.at[pslot, rows[c]],
            send_sem.at[0, c],
            recv_sem.at[pslot, c],
            {"peak": partner},
        )

    def to_far(c, up):
        slot = 0 if up else 2 * reach
        return remote(
            q_own.at[rows[c]],
            q_all.at[slot, rows[c]],
            send_sem.at[1 if up else 2, c],
            recv_sem.at[slot, c],
            {"peak": me + 2 if up else me - 2},
        )

    def relayed(c):
        return remote(
            q_all.at[pslot, rows[c]],
            q_all.at[rslot, rows[c]],
            send_sem.at[3, c],
            recv_sem.at[rslot, c],
            {"peak": ahead},
        )

    for c in range(chunks):
        to_partner(c).start()
    for up in ways:

        @pl.when(inside(me + 2 if up else me - 2, n))
        def _():
            for c in range(chunks):
                to_far(c, up).start()

    here = pl.ds(pl.multiple_of(g * cols, TILE), cols)
    own_w = pltpu.make_async_copy(w_out.at[:, here], wo_all.at[g], local_sem.at[0])
    own_w.start()
    for r, peer in enumerate(others):
        there = pl.ds(pl.multiple_of(peer * cols, TILE), cols)
        remote(
            w_out.at[:, there], wo_all.at[g], w_send.at[r], w_recv.at[r], {"gene": peer}
        ).start()

    loads[2].wait()
    loads[3].wait()
    for c in range(chunks):
        part = pl.ds(c * piece, piece)
        peak_loads[c].wait()
        keys[part] = jnp.dot(pa[part], wk[...], preferred_element_type=jnp.float32).astype(keys.dtype)
        values[part] = jnp.dot(pa[part], wv[...], preferred_element_type=jnp.float32).astype(
            values.dtype
        )
        from_partner(c).wait_recv()

        @pl.when(inside(ahead, n))
        def _():
            relayed(c).start()

    own_part[...] = jnp.zeros_like(own_part)
    span = CHUNK_TILES * TILE
    spans = peak_act.shape[0] // span

    def own_chunk(c, carry):
        at = pl.ds(pl.multiple_of(c * span, span), span)
        masks = [
            allowed_pairs(
                gene_tags, peak_tags, me * chunks + t, me * spans + c, codes[me * chunks + t, me * spans + c]
            )
            for t in range(chunks)
        ]
        heads = head_bias.shape[0]
        dim = keys.shape[1] // heads
        for h in range(heads):
            head = pl.ds(h * dim, dim)
            scores = score(q_own[:, head], keys[at, head])
            weights = gate(scores, head_bias[h], dim)
            weights = jnp.concatenate(
                [
                    jnp.where(masks[t], weights[t * TILE : (t + 1) * TILE], 0.0).astype(jnp.bfloat16)
                    for t in range(chunks)
                ],
                axis=0,
            )
            own_part[:, head] += jnp.dot(
                weights, values[at, head], preferred_element_type=jnp.float32
            )
        return carry

    lax.fori_loop(0, spans, own_chunk, 0)

    for c in range(chunks):
        to_partner(c).wait_send()
    for up in ways:

        @pl.when(inside(me + 2 if up else me - 2, n))
        def _():
            for c in range(chunks):
                to_far(c, up).wait_send()

        @pl.when(inside(me - 2 if up else me + 2, n))
        def _():
            for c in range(chunks):
                to_far(c, up).wait_recv()

    @pl.when(inside(ahead, n))
    def _():
        for c in range(chunks):
            relayed(c).wait_send()

    @pl.when(inside(behind, n))
    def _():
        for c in range(chunks):
            relayed(c).wait_recv()

    own_w.wait()
    for r, peer in enumerate(others):
        there = pl.ds(pl.multiple_of(peer * cols, TILE), cols)
        source = lax.rem(g + gn - 1 - r, gn)
        copy = remote(
            w_out.at[:, there], wo_all.at[source], w_send.at[r], w_recv.at[r], {"gene": peer}
        )
        copy.wait_send()
        copy.wait_recv()


def attend_kernel(
    n, reach, codes, head_bias, gene_tags, peak_tags, q_all, keys, values, parts, total, live, where
):
    me = where[0]
    gene_tiles = q_all.shape[1] // TILE
    peak_rows = keys.shape[0]
    span = CHUNK_TILES * TILE
    spans = peak_rows // span
    heads = head_bias.shape[0]
    dim = keys.shape[1] // heads
    live[0] = 0
    found = jnp.int32(0)
    for slot in range(2 * reach + 1):
        if slot == reach:
            continue
        source = me + slot - reach
        exists = inside(source, n)
        source = jnp.clip(source, 0, n - 1)
        for tile in range(gene_tiles):
            for c in range(spans):
                code = codes[source * gene_tiles + tile, me * spans + c]
                live[found] = (slot * gene_tiles + tile) * spans + c
                found = found + (exists & (code != 0)).astype(jnp.int32)
        total[slot] = jnp.zeros(total.shape[1:], total.dtype)

    def scores_of(i):
        pair = live[i]
        tile = pair // spans
        at = pl.ds(pl.multiple_of((pair % spans) * span, span), span)
        rows = pl.ds(pl.multiple_of((tile % gene_tiles) * TILE, TILE), TILE)
        slot = tile // gene_tiles
        return tuple(
            score(q_all[slot, rows, pl.ds(h * dim, dim)], keys[at, pl.ds(h * dim, dim)])
            for h in range(heads)
        )

    def one_pair(i, scores):
        later = scores_of(jnp.minimum(i + 1, found - 1))
        pair = live[i]
        tile = pair // spans
        c = pair % spans
        slot = tile // gene_tiles
        rows = pl.ds(pl.multiple_of((tile % gene_tiles) * TILE, TILE), TILE)
        at = pl.ds(pl.multiple_of(c * span, span), span)
        gene_tile = (me - reach) * gene_tiles + tile
        chunk = me * spans + c
        allowed = allowed_pairs(gene_tags, peak_tags, gene_tile, chunk, codes[gene_tile, chunk])
        for h in range(heads):
            head = pl.ds(h * dim, dim)
            weights = jnp.where(allowed, gate(scores[h], head_bias[h], dim), 0.0)
            total[slot, rows, head] += jnp.dot(
                weights.astype(jnp.bfloat16), values[at, head], preferred_element_type=jnp.float32
            )
        return later

    @pl.when(found > 0)
    def _():
        lax.fori_loop(0, found, one_pair, scores_of(0))

    for slot in range(2 * reach + 1):
        if slot != reach:
            parts[slot] = total[slot].astype(parts.dtype)


def mix_kernel(
    n,
    gn,
    reach,
    parts,
    own_part,
    wo_all,
    mixed,
    from_up,
    from_down,
    diagonal,
    joined,
    summed,
    attended,
    far_send,
    far_recv,
    near_send,
    near_recv,
    gene_send,
    gene_recv,
):
    me, odd, partner, ahead, behind = places(n)
    g = lax.axis_index("gene")
    chunks = parts.shape[1] // TILE
    pslot = reach + 1 - 2 * odd
    rslot = reach - 1 + 2 * odd
    ways = (True, False) if reach > 1 else ()
    core = g + 1 - 2 * lax.rem(g, 2)
    across = [lax.rem(g + 2 * r, gn) for r in range(1, gn // 2)]
    barrier, count = greet(me, partner, n, [core] + across)
    rows = [pl.ds(c * TILE, TILE) for c in range(chunks)]
    pl.semaphore_wait(barrier, count)

    def diag(c):
        return remote(
            parts.at[rslot, rows[c]],
            diagonal.at[rows[c]],
            near_send.at[0, c],
            near_recv.at[0, c],
            {"peak": behind},
        )

    def join(c):
        return remote(
            joined.at[rows[c]],
            summed.at[rows[c]],
            near_send.at[1, c],
            near_recv.at[1, c],
            {"peak": partner},
        )

    def far(c, up):
        return remote(
            parts.at[2 * reach if up else 0, rows[c]],
            (from_down if up else from_up).at[rows[c]],
            far_send.at[0 if up else 1, c],
            far_recv.at[0 if up else 1, c],
            {"peak": me + 2 if up else me - 2},
        )

    @pl.when(inside(behind, n))
    def _():
        for c in range(chunks):
            diag(c).start()

    for up in ways:

        @pl.when(inside(me + 2 if up else me - 2, n))
        def _():
            for c in range(chunks):
                far(c, up).start()

    for c in range(chunks):

        @pl.when(inside(ahead, n))
        def _():
            diag(c).wait_recv()
            joined[rows[c]] = (
                parts[pslot, rows[c]].astype(jnp.float32) + diagonal[rows[c]].astype(jnp.float32)
            ).astype(joined.dtype)

        @pl.when(jnp.logical_not(inside(ahead, n)))
        def _():
            joined[rows[c]] = parts[pslot, rows[c]]

        join(c).start()

    def gather(c, block, peer, lane):
        return remote(
            attended.at[block, rows[c]],
            attended.at[block, rows[c]],
            gene_send.at[lane, c],
            gene_recv.at[block, c],
            {"gene": peer},
        )

    def finish(c):
        for r, peer in enumerate(across):
            gather(c, peer, peer, 0).wait_recv()
            gather(c, peer, core, len(across) + 1 + r).start()

    def product(c):
        gather(c, core, core, 0).wait_recv()
        for peer in across:
            gather(c, peer + 1 - 2 * lax.rem(peer, 2), core, 0).wait_recv()
        out = jnp.dot(attended[0, rows[c]], wo_all[0], preferred_element_type=jnp.float32)
        for block in range(1, gn):
            out += jnp.dot(
                attended[block, rows[c]], wo_all[block], preferred_element_type=jnp.float32
            )
        mixed[rows[c]] = out.astype(mixed.dtype)

    for c in range(chunks):
        join(c).wait_recv()
        for up in ways:

            @pl.when(inside(me - 2 if up else me + 2, n))
            def _():
                far(c, up).wait_recv()

        total = own_part[rows[c]] + summed[rows[c]].astype(jnp.float32)
        if reach > 1:
            low = jnp.where(inside(me - 2, n), from_down[rows[c]].astype(jnp.float32), 0.0)
            high = jnp.where(inside(me + 2, n), from_up[rows[c]].astype(jnp.float32), 0.0)
            total = total + low + high
        attended[g, rows[c]] = total.astype(attended.dtype)
        gather(c, g, core, 0).start()
        for r, peer in enumerate(across):
            gather(c, g, peer, 1 + r).start()
        if c >= 1:
            finish(c - 1)
    finish(chunks - 1)
    for c in range(chunks):
        product(c)

    for c in range(chunks):
        join(c).wait_send()
        for lane in range(1 + 2 * len(across)):
            gather(c, g, core, lane).wait_send()
    for up in ways:

        @pl.when(inside(me + 2 if up else me - 2, n))
        def _():
            for c in range(chunks):
                far(c, up).wait_send()

    @pl.when(inside(behind, n))
    def _():
        for c in range(chunks):
            diag(c).wait_send()


def plan_kernel(gene_tiles, peak_tiles, block_mask, gene_tags, peak_tags, codes, far):
    rows, cols = block_mask.shape
    first = jnp.transpose(peak_tags[...])[:1, :]
    last = jnp.transpose(peak_tags[...])[TILE - 1 :, :]
    live = (
        (block_mask[...] == 1)
        & (gene_tags[:, :1] <= last)
        & (first <= gene_tags[:, TILE - 1 :])
    ).astype(jnp.float32)
    tile = lax.broadcasted_iota(jnp.int32, (cols, codes.shape[1]), 0)
    chunk = lax.broadcasted_iota(jnp.int32, (cols, codes.shape[1]), 1)
    bit = jnp.left_shift(1, lax.rem(tile, CHUNK_TILES))
    spread = jnp.where(lax.div(tile, CHUNK_TILES) == chunk, bit, 0).astype(jnp.float32)
    codes[...] = jnp.dot(live, spread, preferred_element_type=jnp.float32).astype(jnp.int32)
    gene_shard = lax.div(lax.broadcasted_iota(jnp.int32, (rows, cols), 0), gene_tiles)
    peak_shard = lax.div(lax.broadcasted_iota(jnp.int32, (rows, cols), 1), peak_tiles)
    apart = jnp.abs(gene_shard - peak_shard) > 1
    far[0, 0] = (jnp.sum(jnp.where(apart, live, 0.0)) > 0.5).astype(jnp.int32)


def layer(
    reach, n, gn, gene_act, peak_act, w_query, w_key, w_value, w_out, head_bias, where, codes,
    gene_tags, peak_tags,
):
    gene_rows, peak_rows = gene_act.shape[0], peak_act.shape[0]
    width = w_query.shape[1]
    cols = w_out.shape[1] // gn
    chunks = gene_rows // TILE
    slots = 2 * reach + 1
    dtype = gene_act.dtype
    in_hbm = pl.BlockSpec(memory_space=pltpu.HBM)
    in_vmem = pl.BlockSpec(memory_space=pltpu.VMEM)
    in_smem = pl.BlockSpec(memory_space=pltpu.SMEM)

    q_all, keys, values, wo_all, own_part = pl.pallas_call(
        functools.partial(exchange_kernel, n, gn, reach),
        out_shape=(
            jax.ShapeDtypeStruct((slots, gene_rows, width), dtype),
            jax.ShapeDtypeStruct((peak_rows, width), dtype),
            jax.ShapeDtypeStruct((peak_rows, width), dtype),
            jax.ShapeDtypeStruct((gn, w_out.shape[0], cols), dtype),
            jax.ShapeDtypeStruct((gene_rows, width), jnp.float32),
        ),
        in_specs=[in_hbm] * 6 + [in_smem] * 2 + [in_vmem] * 2,
        out_specs=(in_vmem,) * 5,
        scratch_shapes=[
            pltpu.VMEM(gene_act.shape, dtype),
            pltpu.VMEM(peak_act.shape, dtype),
            pltpu.VMEM(w_query.shape, dtype),
            pltpu.VMEM(w_key.shape, dtype),
            pltpu.VMEM(w_value.shape, dtype),
            pltpu.VMEM((gene_rows, width), dtype),
            pltpu.SemaphoreType.DMA((4 + chunks,)),
            pltpu.SemaphoreType.DMA((1,)),
            pltpu.SemaphoreType.DMA((4, chunks)),
            pltpu.SemaphoreType.DMA((slots, chunks)),
            pltpu.SemaphoreType.DMA((gn - 1,)),
            pltpu.SemaphoreType.DMA((gn - 1,)),
        ],
        compiler_params=pltpu.CompilerParams(
            collective_id=2 * reach, has_side_effects=True, vmem_limit_bytes=VMEM_LIMIT
        ),
    )(gene_act, peak_act, w_query, w_key, w_value, w_out, head_bias, codes, gene_tags, peak_tags)

    def attend(where, *refs):
        attend_kernel(n, reach, *refs, where)

    parts = pl.pallas_call(
        attend,
        out_shape=jax.ShapeDtypeStruct((slots, gene_rows, width), dtype),
        in_specs=[in_smem] * 3 + [in_vmem] * 5,
        out_specs=in_vmem,
        scratch_shapes=[
            pltpu.VMEM((slots, gene_rows, width), jnp.float32),
            pltpu.SMEM((slots * chunks * (peak_rows // TILE // CHUNK_TILES) + 1,), jnp.int32),
        ],
        compiler_params=pltpu.CompilerParams(vmem_limit_bytes=VMEM_LIMIT),
    )(where, codes, head_bias, gene_tags, peak_tags, q_all, keys, values)

    return pl.pallas_call(
        functools.partial(mix_kernel, n, gn, reach),
        out_shape=jax.ShapeDtypeStruct((gene_rows, cols), dtype),
        in_specs=[in_vmem] * 3,
        out_specs=in_vmem,
        scratch_shapes=[pltpu.VMEM((gene_rows, width), dtype)] * 5
        + [
            pltpu.VMEM((gn, gene_rows, width), dtype),
            pltpu.SemaphoreType.DMA((2, chunks)),
            pltpu.SemaphoreType.DMA((2, chunks)),
            pltpu.SemaphoreType.DMA((2, chunks)),
            pltpu.SemaphoreType.DMA((2, chunks)),
            pltpu.SemaphoreType.DMA((gn, chunks)),
            pltpu.SemaphoreType.DMA((gn, chunks)),
        ],
        compiler_params=pltpu.CompilerParams(
            collective_id=2 * reach + 1, has_side_effects=True, vmem_limit_bytes=VMEM_LIMIT
        ),
    )(parts, own_part, wo_all)


def on_device(
    gene_act,
    peak_act,
    w_query,
    w_key,
    w_value,
    w_out,
    head_bias,
    block_mask,
    gene_chrom,
    peak_chrom,
):
    n, gn = lax.axis_size("peak"), lax.axis_size("gene")
    in_vmem = pl.BlockSpec(memory_space=pltpu.VMEM)
    gene_tags = gene_chrom.reshape(-1, TILE)
    peak_tags = peak_chrom.reshape(-1, TILE)
    rows, cols = block_mask.shape
    code_cols = -(-(cols // CHUNK_TILES) // TILE) * TILE
    codes, far = pl.pallas_call(
        functools.partial(plan_kernel, rows // n, cols // n),
        out_shape=(
            jax.ShapeDtypeStruct((rows, code_cols), jnp.int32),
            jax.ShapeDtypeStruct((1, 1), jnp.int32),
        ),
        in_specs=[in_vmem] * 3,
        out_specs=(in_vmem, pl.BlockSpec(memory_space=pltpu.SMEM)),
        compiler_params=pltpu.CompilerParams(vmem_limit_bytes=VMEM_LIMIT),
    )(block_mask, gene_tags, peak_tags)
    where = lax.axis_index("peak").astype(jnp.int32).reshape(1)
    operands = (
        gene_act, peak_act, w_query, w_key, w_value, w_out, head_bias, where, codes, gene_tags,
        peak_tags,
    )
    return lax.cond(
        far[0, 0] > 0,
        functools.partial(layer, REACH, n, gn),
        functools.partial(layer, 1, n, gn),
        *operands,
    )


def solution(mesh):
    placed = (
        P("peak", None),
        P("peak", None),
        P(None, "gene"),
        P(None, "gene"),
        P(None, "gene"),
        P("gene", None),
        P("gene"),
        P(),
        P(),
        P(),
    )
    return jax.shard_map(
        on_device, mesh=mesh, in_specs=placed, out_specs=P("peak", "gene"), check_vma=False
    )
```

```python
import functools
import math

import jax
import jax.numpy as jnp
from jax import lax
from jax.experimental import pallas as pl
from jax.experimental.pallas import tpu as pltpu
from jax.sharding import PartitionSpec as P

TILE = 128
REACH = 2
CHUNK_TILES = 4
MIX_ROWS = 64
LOG2E = 1.4426950408889634
MESH = pl.DeviceIdType.MESH
VMEM_LIMIT = 48 * 1024 * 1024


def remote(src, dst, send_sem, recv_sem, where):
    return pltpu.make_async_remote_copy(
        src_ref=src,
        dst_ref=dst,
        send_sem=send_sem,
        recv_sem=recv_sem,
        device_id=where,
        device_id_type=MESH,
    )


def places(n):
    me = lax.axis_index("peak")
    odd = lax.rem(me, 2)
    partner = me + 1 - 2 * odd
    ahead = me + 2 - 4 * odd
    behind = me - 2 + 4 * odd
    return me, odd, partner, ahead, behind


def inside(shard, n):
    return (shard >= 0) & (shard < n)


def greet(me, partner, n, gene_peers):
    barrier = pltpu.get_barrier_semaphore()
    pl.semaphore_signal(barrier, inc=1, device_id={"peak": partner}, device_id_type=MESH)
    for far in (me + 2, me - 2):

        @pl.when(inside(far, n))
        def _():
            pl.semaphore_signal(barrier, inc=1, device_id={"peak": far}, device_id_type=MESH)

    for peer in gene_peers:
        pl.semaphore_signal(barrier, inc=1, device_id={"gene": peer}, device_id_type=MESH)
    count = (
        1
        + len(gene_peers)
        + inside(me + 2, n).astype(jnp.int32)
        + inside(me - 2, n).astype(jnp.int32)
    )
    return barrier, count


def score(queries, keys):
    return lax.dot_general(
        queries, keys, (((1,), (1,)), ((), ())), preferred_element_type=jnp.float32
    )


def gate(scores, bias, dim):
    grown = jnp.exp2(scores * (-LOG2E / math.sqrt(dim)) - bias * LOG2E)
    return pl.reciprocal(1.0 + grown, approx=True)


def allowed_pairs(gene_tags, peak_tags, gene_tile, chunk, code):
    row = gene_tags[pl.ds(gene_tile, 1), :]
    gene_tag = jnp.transpose(jnp.broadcast_to(row, (TILE, TILE)))
    allowed = []
    for t in range(CHUNK_TILES):
        tags = peak_tags[pl.ds(chunk * CHUNK_TILES + t, 1), :]
        tags = jnp.where((code >> t) & 1 == 1, tags, -1)
        allowed.append(gene_tag == tags)
    return jnp.concatenate(allowed, axis=1)


def exchange_kernel(
    n,
    gn,
    reach,
    gene_act,
    peak_act,
    w_query,
    w_key,
    w_value,
    w_out,
    head_bias,
    codes,
    gene_tags,
    peak_tags,
    q_all,
    keys,
    values,
    wo_all,
    own_part,
    ga,
    pa,
    wq,
    wk,
    wv,
    q_own,
    load_sem,
    local_sem,
    send_sem,
    recv_sem,
    w_send,
    w_recv,
):
    me, odd, partner, ahead, behind = places(n)
    g = lax.axis_index("gene")
    chunks = gene_act.shape[0] // TILE
    piece = peak_act.shape[0] // chunks
    cols = w_out.shape[1] // gn
    pslot = reach + 1 - 2 * odd
    rslot = reach - 1 + 2 * odd
    ways = (True, False) if reach > 1 else ()
    others = [lax.rem(g + r, gn) for r in range(1, gn)]
    barrier, count = greet(me, partner, n, others)

    loads = [
        pltpu.make_async_copy(src, dst, load_sem.at[i])
        for i, (src, dst) in enumerate(
            ((gene_act, ga), (w_query, wq), (w_key, wk), (w_value, wv))
        )
    ]
    for load in loads:
        load.start()
    peak_loads = [
        pltpu.make_async_copy(
            peak_act.at[pl.ds(c * piece, piece)], pa.at[pl.ds(c * piece, piece)], load_sem.at[4 + c]
        )
        for c in range(chunks)
    ]
    for load in peak_loads:
        load.start()
    loads[0].wait()
    loads[1].wait()
    rows = [pl.ds(c * TILE, TILE) for c in range(chunks)]
    q_own[...] = jnp.dot(ga[...], wq[...], preferred_element_type=jnp.float32).astype(q_own.dtype)
    pl.semaphore_wait(barrier, count)

    def to_partner(c):
        return remote(
            q_own.at[rows[c]],
            q_all.at[rslot, rows[c]],
            send_sem.at[0, c],
            recv_sem.at[rslot, c],
            {"peak": partner},
        )

    def from_partner(c):
        return remote(
            q_own.at[rows[c]],
            q_all.at[pslot, rows[c]],
            send_sem.at[0, c],
            recv_sem.at[pslot, c],
            {"peak": partner},
        )

    def to_far(c, up):
        slot = 0 if up else 2 * reach
        return remote(
            q_own.at[rows[c]],
            q_all.at[slot, rows[c]],
            send_sem.at[1 if up else 2, c],
            recv_sem.at[slot, c],
            {"peak": me + 2 if up else me - 2},
        )

    def relayed(c):
        return remote(
            q_all.at[pslot, rows[c]],
            q_all.at[rslot, rows[c]],
            send_sem.at[3, c],
            recv_sem.at[rslot, c],
            {"peak": ahead},
        )

    for c in range(chunks):
        to_partner(c).start()
    for up in ways:

        @pl.when(inside(me + 2 if up else me - 2, n))
        def _():
            for c in range(chunks):
                to_far(c, up).start()

    here = pl.ds(pl.multiple_of(g * cols, TILE), cols)
    own_w = pltpu.make_async_copy(w_out.at[:, here], wo_all.at[g], local_sem.at[0])
    own_w.start()
    for r, peer in enumerate(others):
        there = pl.ds(pl.multiple_of(peer * cols, TILE), cols)
        remote(
            w_out.at[:, there], wo_all.at[g], w_send.at[r], w_recv.at[r], {"gene": peer}
        ).start()

    loads[2].wait()
    loads[3].wait()
    for c in range(chunks):
        part = pl.ds(c * piece, piece)
        peak_loads[c].wait()
        keys[part] = jnp.dot(pa[part], wk[...], preferred_element_type=jnp.float32).astype(keys.dtype)
        values[part] = jnp.dot(pa[part], wv[...], preferred_element_type=jnp.float32).astype(
            values.dtype
        )
        from_partner(c).wait_recv()

        @pl.when(inside(ahead, n))
        def _():
            relayed(c).start()

    own_part[...] = jnp.zeros_like(own_part)
    span = CHUNK_TILES * TILE
    spans = peak_act.shape[0] // span

    def own_chunk(c, carry):
        at = pl.ds(pl.multiple_of(c * span, span), span)
        masks = [
            allowed_pairs(
                gene_tags, peak_tags, me * chunks + t, me * spans + c, codes[me * chunks + t, me * spans + c]
            )
            for t in range(chunks)
        ]
        heads = head_bias.shape[0]
        dim = keys.shape[1] // heads
        for h in range(heads):
            head = pl.ds(h * dim, dim)
            scores = score(q_own[:, head], keys[at, head])
            weights = gate(scores, head_bias[h], dim)
            weights = jnp.concatenate(
                [
                    jnp.where(masks[t], weights[t * TILE : (t + 1) * TILE], 0.0).astype(jnp.bfloat16)
                    for t in range(chunks)
                ],
                axis=0,
            )
            own_part[:, head] += jnp.dot(
                weights, values[at, head], preferred_element_type=jnp.float32
            )
        return carry

    lax.fori_loop(0, spans, own_chunk, 0)

    for c in range(chunks):
        to_partner(c).wait_send()
    for up in ways:

        @pl.when(inside(me + 2 if up else me - 2, n))
        def _():
            for c in range(chunks):
                to_far(c, up).wait_send()

        @pl.when(inside(me - 2 if up else me + 2, n))
        def _():
            for c in range(chunks):
                to_far(c, up).wait_recv()

    @pl.when(inside(ahead, n))
    def _():
        for c in range(chunks):
            relayed(c).wait_send()

    @pl.when(inside(behind, n))
    def _():
        for c in range(chunks):
            relayed(c).wait_recv()

    own_w.wait()
    for r, peer in enumerate(others):
        there = pl.ds(pl.multiple_of(peer * cols, TILE), cols)
        source = lax.rem(g + gn - 1 - r, gn)
        copy = remote(
            w_out.at[:, there], wo_all.at[source], w_send.at[r], w_recv.at[r], {"gene": peer}
        )
        copy.wait_send()
        copy.wait_recv()


def attend_kernel(
    n, reach, codes, head_bias, gene_tags, peak_tags, q_all, keys, values, parts, total, live, where
):
    me = where[0]
    gene_tiles = q_all.shape[1] // TILE
    peak_rows = keys.shape[0]
    span = CHUNK_TILES * TILE
    spans = peak_rows // span
    heads = head_bias.shape[0]
    dim = keys.shape[1] // heads
    live[0] = 0
    found = jnp.int32(0)
    for slot in range(2 * reach + 1):
        if slot == reach:
            continue
        source = me + slot - reach
        exists = inside(source, n)
        source = jnp.clip(source, 0, n - 1)
        for tile in range(gene_tiles):
            for c in range(spans):
                code = codes[source * gene_tiles + tile, me * spans + c]
                live[found] = (slot * gene_tiles + tile) * spans + c
                found = found + (exists & (code != 0)).astype(jnp.int32)
        total[slot] = jnp.zeros(total.shape[1:], total.dtype)

    def scores_of(i):
        pair = live[i]
        tile = pair // spans
        at = pl.ds(pl.multiple_of((pair % spans) * span, span), span)
        rows = pl.ds(pl.multiple_of((tile % gene_tiles) * TILE, TILE), TILE)
        slot = tile // gene_tiles
        return tuple(
            score(q_all[slot, rows, pl.ds(h * dim, dim)], keys[at, pl.ds(h * dim, dim)])
            for h in range(heads)
        )

    def one_pair(i, scores):
        later = scores_of(jnp.minimum(i + 1, found - 1))
        pair = live[i]
        tile = pair // spans
        c = pair % spans
        slot = tile // gene_tiles
        rows = pl.ds(pl.multiple_of((tile % gene_tiles) * TILE, TILE), TILE)
        at = pl.ds(pl.multiple_of(c * span, span), span)
        gene_tile = (me - reach) * gene_tiles + tile
        chunk = me * spans + c
        allowed = allowed_pairs(gene_tags, peak_tags, gene_tile, chunk, codes[gene_tile, chunk])
        for h in range(heads):
            head = pl.ds(h * dim, dim)
            weights = jnp.where(allowed, gate(scores[h], head_bias[h], dim), 0.0)
            total[slot, rows, head] += jnp.dot(
                weights.astype(jnp.bfloat16), values[at, head], preferred_element_type=jnp.float32
            )
        return later

    @pl.when(found > 0)
    def _():
        lax.fori_loop(0, found, one_pair, scores_of(0))

    for slot in range(2 * reach + 1):
        if slot != reach:
            parts[slot] = total[slot].astype(parts.dtype)


def mix_kernel(
    n,
    gn,
    reach,
    parts,
    own_part,
    wo_all,
    mixed,
    from_up,
    from_down,
    diagonal,
    joined,
    summed,
    attended,
    far_send,
    far_recv,
    near_send,
    near_recv,
    gene_send,
    gene_recv,
):
    me, odd, partner, ahead, behind = places(n)
    g = lax.axis_index("gene")
    chunks = parts.shape[1] // MIX_ROWS
    pslot = reach + 1 - 2 * odd
    rslot = reach - 1 + 2 * odd
    ways = (True, False) if reach > 1 else ()
    core = g + 1 - 2 * lax.rem(g, 2)
    across = [lax.rem(g + 2 * r, gn) for r in range(1, gn // 2)]
    barrier, count = greet(me, partner, n, [core] + across)
    rows = [pl.ds(c * MIX_ROWS, MIX_ROWS) for c in range(chunks)]
    group = TILE // MIX_ROWS
    pl.semaphore_wait(barrier, count)

    def diag(c):
        return remote(
            parts.at[rslot, rows[c]],
            diagonal.at[rows[c]],
            near_send.at[0, c],
            near_recv.at[0, c],
            {"peak": behind},
        )

    def join(c):
        return remote(
            joined.at[rows[c]],
            summed.at[rows[c]],
            near_send.at[1, c],
            near_recv.at[1, c],
            {"peak": partner},
        )

    def far(c, up):
        return remote(
            parts.at[2 * reach if up else 0, rows[c]],
            (from_down if up else from_up).at[rows[c]],
            far_send.at[0 if up else 1, c],
            far_recv.at[0 if up else 1, c],
            {"peak": me + 2 if up else me - 2},
        )

    @pl.when(inside(behind, n))
    def _():
        for c in range(chunks):
            diag(c).start()

    for up in ways:

        @pl.when(inside(me + 2 if up else me - 2, n))
        def _():
            for c in range(chunks):
                far(c, up).start()

    for c in range(chunks):

        @pl.when(inside(ahead, n))
        def _():
            diag(c).wait_recv()
            joined[rows[c]] = (
                parts[pslot, rows[c]].astype(jnp.float32) + diagonal[rows[c]].astype(jnp.float32)
            ).astype(joined.dtype)

        @pl.when(jnp.logical_not(inside(ahead, n)))
        def _():
            joined[rows[c]] = parts[pslot, rows[c]]

        join(c).start()

    def gather(c, block, peer, lane):
        return remote(
            attended.at[block, rows[c]],
            attended.at[block, rows[c]],
            gene_send.at[lane, c],
            gene_recv.at[block, c],
            {"gene": peer},
        )

    def finish(c):
        for r, peer in enumerate(across):
            gather(c, peer, peer, 0).wait_recv()
            gather(c, peer, core, len(across) + 1 + r).start()

    def product(t):
        for c in range(t * group, (t + 1) * group):
            gather(c, core, core, 0).wait_recv()
            for peer in across:
                gather(c, peer + 1 - 2 * lax.rem(peer, 2), core, 0).wait_recv()
        at = pl.ds(t * TILE, TILE)
        out = jnp.dot(attended[0, at], wo_all[0], preferred_element_type=jnp.float32)
        for block in range(1, gn):
            out += jnp.dot(attended[block, at], wo_all[block], preferred_element_type=jnp.float32)
        mixed[at] = out.astype(mixed.dtype)

    done = 0
    for c in range(chunks):
        join(c).wait_recv()
        for up in ways:

            @pl.when(inside(me - 2 if up else me + 2, n))
            def _():
                far(c, up).wait_recv()

        total = own_part[rows[c]] + summed[rows[c]].astype(jnp.float32)
        if reach > 1:
            low = jnp.where(inside(me - 2, n), from_down[rows[c]].astype(jnp.float32), 0.0)
            high = jnp.where(inside(me + 2, n), from_up[rows[c]].astype(jnp.float32), 0.0)
            total = total + low + high
        attended[g, rows[c]] = total.astype(attended.dtype)
        gather(c, g, core, 0).start()
        for r, peer in enumerate(across):
            gather(c, g, peer, 1 + r).start()
        if c >= 1:
            finish(c - 1)
        if c % group == group - 1 and c >= 2 * group + 1:
            product(done)
            done += 1
    finish(chunks - 1)
    for t in range(done, chunks // group):
        product(t)

    for c in range(chunks):
        join(c).wait_send()
        for lane in range(1 + 2 * len(across)):
            gather(c, g, core, lane).wait_send()
    for up in ways:

        @pl.when(inside(me + 2 if up else me - 2, n))
        def _():
            for c in range(chunks):
                far(c, up).wait_send()

    @pl.when(inside(behind, n))
    def _():
        for c in range(chunks):
            diag(c).wait_send()


def plan_kernel(gene_tiles, peak_tiles, block_mask, gene_tags, peak_tags, codes, far):
    rows, cols = block_mask.shape
    first = jnp.transpose(peak_tags[...])[:1, :]
    last = jnp.transpose(peak_tags[...])[TILE - 1 :, :]
    live = (
        (block_mask[...] == 1)
        & (gene_tags[:, :1] <= last)
        & (first <= gene_tags[:, TILE - 1 :])
    ).astype(jnp.float32)
    tile = lax.broadcasted_iota(jnp.int32, (cols, codes.shape[1]), 0)
    chunk = lax.broadcasted_iota(jnp.int32, (cols, codes.shape[1]), 1)
    bit = jnp.left_shift(1, lax.rem(tile, CHUNK_TILES))
    spread = jnp.where(lax.div(tile, CHUNK_TILES) == chunk, bit, 0).astype(jnp.float32)
    codes[...] = jnp.dot(live, spread, preferred_element_type=jnp.float32).astype(jnp.int32)
    gene_shard = lax.div(lax.broadcasted_iota(jnp.int32, (rows, cols), 0), gene_tiles)
    peak_shard = lax.div(lax.broadcasted_iota(jnp.int32, (rows, cols), 1), peak_tiles)
    apart = jnp.abs(gene_shard - peak_shard) > 1
    far[0, 0] = (jnp.sum(jnp.where(apart, live, 0.0)) > 0.5).astype(jnp.int32)


def layer(
    reach, n, gn, gene_act, peak_act, w_query, w_key, w_value, w_out, head_bias, where, codes,
    gene_tags, peak_tags,
):
    gene_rows, peak_rows = gene_act.shape[0], peak_act.shape[0]
    width = w_query.shape[1]
    cols = w_out.shape[1] // gn
    chunks = gene_rows // TILE
    slots = 2 * reach + 1
    dtype = gene_act.dtype
    in_hbm = pl.BlockSpec(memory_space=pltpu.HBM)
    in_vmem = pl.BlockSpec(memory_space=pltpu.VMEM)
    in_smem = pl.BlockSpec(memory_space=pltpu.SMEM)

    q_all, keys, values, wo_all, own_part = pl.pallas_call(
        functools.partial(exchange_kernel, n, gn, reach),
        out_shape=(
            jax.ShapeDtypeStruct((slots, gene_rows, width), dtype),
            jax.ShapeDtypeStruct((peak_rows, width), dtype),
            jax.ShapeDtypeStruct((peak_rows, width), dtype),
            jax.ShapeDtypeStruct((gn, w_out.shape[0], cols), dtype),
            jax.ShapeDtypeStruct((gene_rows, width), jnp.float32),
        ),
        in_specs=[in_hbm] * 6 + [in_smem] * 2 + [in_vmem] * 2,
        out_specs=(in_vmem,) * 5,
        scratch_shapes=[
            pltpu.VMEM(gene_act.shape, dtype),
            pltpu.VMEM(peak_act.shape, dtype),
            pltpu.VMEM(w_query.shape, dtype),
            pltpu.VMEM(w_key.shape, dtype),
            pltpu.VMEM(w_value.shape, dtype),
            pltpu.VMEM((gene_rows, width), dtype),
            pltpu.SemaphoreType.DMA((4 + chunks,)),
            pltpu.SemaphoreType.DMA((1,)),
            pltpu.SemaphoreType.DMA((4, chunks)),
            pltpu.SemaphoreType.DMA((slots, chunks)),
            pltpu.SemaphoreType.DMA((gn - 1,)),
            pltpu.SemaphoreType.DMA((gn - 1,)),
        ],
        compiler_params=pltpu.CompilerParams(
            collective_id=2 * reach, has_side_effects=True, vmem_limit_bytes=VMEM_LIMIT
        ),
    )(gene_act, peak_act, w_query, w_key, w_value, w_out, head_bias, codes, gene_tags, peak_tags)

    def attend(where, *refs):
        attend_kernel(n, reach, *refs, where)

    parts = pl.pallas_call(
        attend,
        out_shape=jax.ShapeDtypeStruct((slots, gene_rows, width), dtype),
        in_specs=[in_smem] * 3 + [in_vmem] * 5,
        out_specs=in_vmem,
        scratch_shapes=[
            pltpu.VMEM((slots, gene_rows, width), jnp.float32),
            pltpu.SMEM((slots * chunks * (peak_rows // TILE // CHUNK_TILES) + 1,), jnp.int32),
        ],
        compiler_params=pltpu.CompilerParams(vmem_limit_bytes=VMEM_LIMIT),
    )(where, codes, head_bias, gene_tags, peak_tags, q_all, keys, values)

    return pl.pallas_call(
        functools.partial(mix_kernel, n, gn, reach),
        out_shape=jax.ShapeDtypeStruct((gene_rows, cols), dtype),
        in_specs=[in_vmem] * 3,
        out_specs=in_vmem,
        scratch_shapes=[pltpu.VMEM((gene_rows, width), dtype)] * 5
        + [
            pltpu.VMEM((gn, gene_rows, width), dtype),
            pltpu.SemaphoreType.DMA((2, gene_rows // MIX_ROWS)),
            pltpu.SemaphoreType.DMA((2, gene_rows // MIX_ROWS)),
            pltpu.SemaphoreType.DMA((2, gene_rows // MIX_ROWS)),
            pltpu.SemaphoreType.DMA((2, gene_rows // MIX_ROWS)),
            pltpu.SemaphoreType.DMA((gn, gene_rows // MIX_ROWS)),
            pltpu.SemaphoreType.DMA((gn, gene_rows // MIX_ROWS)),
        ],
        compiler_params=pltpu.CompilerParams(
            collective_id=2 * reach + 1, has_side_effects=True, vmem_limit_bytes=VMEM_LIMIT
        ),
    )(parts, own_part, wo_all)


def on_device(
    gene_act,
    peak_act,
    w_query,
    w_key,
    w_value,
    w_out,
    head_bias,
    block_mask,
    gene_chrom,
    peak_chrom,
):
    n, gn = lax.axis_size("peak"), lax.axis_size("gene")
    in_vmem = pl.BlockSpec(memory_space=pltpu.VMEM)
    gene_tags = gene_chrom.reshape(-1, TILE)
    peak_tags = peak_chrom.reshape(-1, TILE)
    rows, cols = block_mask.shape
    code_cols = -(-(cols // CHUNK_TILES) // TILE) * TILE
    codes, far = pl.pallas_call(
        functools.partial(plan_kernel, rows // n, cols // n),
        out_shape=(
            jax.ShapeDtypeStruct((rows, code_cols), jnp.int32),
            jax.ShapeDtypeStruct((1, 1), jnp.int32),
        ),
        in_specs=[in_vmem] * 3,
        out_specs=(in_vmem, pl.BlockSpec(memory_space=pltpu.SMEM)),
        compiler_params=pltpu.CompilerParams(vmem_limit_bytes=VMEM_LIMIT),
    )(block_mask, gene_tags, peak_tags)
    where = lax.axis_index("peak").astype(jnp.int32).reshape(1)
    operands = (
        gene_act, peak_act, w_query, w_key, w_value, w_out, head_bias, where, codes, gene_tags,
        peak_tags,
    )
    return lax.cond(
        far[0, 0] > 0,
        functools.partial(layer, REACH, n, gn),
        functools.partial(layer, 1, n, gn),
        *operands,
    )


def solution(mesh):
    placed = (
        P("peak", None),
        P("peak", None),
        P(None, "gene"),
        P(None, "gene"),
        P(None, "gene"),
        P("gene", None),
        P("gene"),
        P(),
        P(),
        P(),
    )
    return jax.shard_map(
        on_device, mesh=mesh, in_specs=placed, out_specs=P("peak", "gene"), check_vma=False
    )
```
